32 devices in a mesh: gx: 8 (over y, x, core), gy: 4 (over z).
Axes of the slice: x: 2, y: 2, z: 4, core: 2. Of those that a mesh axis runs over, the one named last changes fastest.
Arguments:
- tokens: bfloat16 [256, 2, 4096], P('gy', None, 'gx'), may hold values from -48 to 48
- gains: float32 [3, 4096], P(None, 'gx'), may hold values from 0.1 to 1.9
- w_qkv: bfloat16 [4096, 3, 4096], P('gx', None, 'gy'), may hold values from -0.09375 to 0.09375
- w_self_out: bfloat16 [4096, 4096], P('gy', 'gx'), may hold values from -0.09375 to 0.09375
- w_cross_q: bfloat16 [4096, 4096], P('gx', 'gy'), may hold values from -0.09375 to 0.09375
- w_cross_out: bfloat16 [4096, 4096], P('gy', 'gx'), may hold values from -0.09375 to 0.09375
- w_ffn_in: bfloat16 [4096, 2, 16384], P('gx', None, 'gy'), may hold values from -0.09375 to 0.09375
- w_ffn_out: bfloat16 [16384, 4096], P('gy', 'gx'), may hold values from -0.046875 to 0.046875
- self_keys: bfloat16 [256, 32, 4096], P(('gx', 'gy')), may hold values from -6 to 6
- self_values: bfloat16 [256, 32, 4096], P(('gx', 'gy')), may hold values from -6 to 6
- cross_keys: bfloat16 [256, 128, 4096], P(('gx', 'gy')), may hold values from -6 to 6
- cross_values: bfloat16 [256, 128, 4096], P(('gx', 'gy')), may hold values from -6 to 6
- positions: int32 [256], P(('gx', 'gy')), may hold values from 1 to 32
- src_len: int32 [256], P(('gx', 'gy')), may hold values from 1 to 128, 20480 in all
Outputs:
- layer_out: bfloat16 [256, 2, 4096], P('gy', None, 'gx')
The draws below stay inside these ranges and needn't reach their ends.
Inputs may be any that keep to these rules, and one draw needn't show every extreme that they name: `positions`: the number of filled cache slots of a row; the row's new tokens follow them. `src_len`: some row has exactly 128 source positions.
All inputs are finite; a program needn't handle non-finite values. No bound on the sum of `src_len` on one device may be relied on, other than what follows from the above.
Results may differ from the reference program's by a relative error of at most 0.023.
Values may be sent and summed in bfloat16 or wider, within the bound.
A program may use at most 192 MiB of HBM per device.

```python
import math
import jax
import jax.numpy as jnp
import numpy as np
from jax import lax

D = 4096
FF = 16384
HEADS = 16
HEAD_DIM = 256
NEW = 2
CACHE = 32
SRC = 128
HD = 4096
ROWS = 256
N_GX = 8


def draw_tokens(key, part):
    first, second, third = jax.random.split(jax.random.fold_in(key, 17), 3)
    row_scale = jnp.exp(jax.random.uniform(second, (ROWS, NEW, 1), jnp.float32, math.log(0.3), math.log(3.0)))
    column_scale = jnp.exp(jax.random.uniform(third, (1, 1, D), jnp.float32, math.log(0.4), math.log(4.0)))
    base = jnp.clip(jax.random.normal(first, (ROWS, NEW, D), jnp.float32), -4.0, 4.0)
    return (base * row_scale * column_scale).astype(jnp.bfloat16)


def plant(drawn, own_key, smallest, top_value):
    spot = [jax.random.randint(jax.random.fold_in(own_key, axis), (), 0, length) for axis, length in enumerate(drawn.shape)]
    longest = drawn.shape.index(max(drawn.shape))
    beside = spot[:longest] + [(spot[longest] + 1) % drawn.shape[longest]] + spot[longest + 1:]
    return drawn.at[tuple(spot)].set(smallest).at[tuple(beside)].set(top_value)


def block_levels(stream_key, dims, cuts, low, top_value):
    level, own = 1.0, jax.random.fold_in(stream_key, 6)
    for dim, blocks in cuts:
        draws = jnp.exp(jax.random.uniform(jax.random.fold_in(own, dim), (blocks,), jnp.float32, low / len(cuts), top_value / len(cuts)))
        level = level * jnp.repeat(draws, dims[dim] // blocks).reshape([-1 if axis == dim else 1 for axis in range(len(dims))])
    return level


def split_up(amount, total, bound, skew):
    loads = [(1 << 20) // math.isqrt(grade ** skew) + 1 for grade in range(2, amount + 1)]
    rest, given = total - bound - (amount - 1), [1] * (amount - 1)
    while rest > 0:
        movable = [i for i in range(amount - 1) if given[i] < bound]
        pool, remaining = sum([loads[i] for i in movable]), rest
        for i in movable:
            more = min(bound - given[i], max(1, remaining * loads[i] // pool), rest)
            given[i] = given[i] + more
            rest = rest - more
    return np.array([bound] + given)


def uneven_parts(rng, amount, total, bound, lean):
    if amount == 2:
        one = jax.random.randint(rng, (), max(1, total - bound), min(bound, total - 1) + 1)
        return jnp.stack([one, total - one])
    sizes = jnp.asarray(split_up(amount, total, bound, lean), jnp.int32)
    pairs = (amount - 1) // 2
    donor, sink = sizes[1:1 + 2 * pairs:2], sizes[2:2 + 2 * pairs:2]
    room = jnp.minimum(donor - 1, bound - sink)
    passed = jax.random.randint(jax.random.fold_in(rng, 1), (pairs,), 0, 1 << 20) % (room + 1)
    sizes = sizes.at[1:1 + 2 * pairs:2].set(donor - passed).at[2:2 + 2 * pairs:2].set(sink + passed)
    return sizes[jax.random.permutation(jax.random.fold_in(rng, 2), amount)]


def noise(own_key, dims, deviation, bound, cuts=(), kind=jnp.bfloat16):
    gain = block_levels(own_key, dims, cuts, -0.22, 0.18) if cuts else 1.0
    array = jax.random.normal(own_key, dims, jnp.float32) * deviation * gain
    return jnp.minimum(jnp.maximum(array, -bound), bound).astype(kind)


def setup_inputs(seed: int = 0) -> dict:
    streams_of = jax.random.split(jax.random.key(seed), 15)
    return {
        "tokens": draw_tokens(jax.random.fold_in(streams_of[14], 71), 0),
        "gains": jnp.clip(1.0 + 0.18 * jax.random.normal(streams_of[1], (3, D), jnp.float32), 0.1, 1.9),
        "w_qkv": noise(streams_of[2], (D, 3, HD), D ** -0.5, 0.09375, ((0, 8), (2, 4))),
        "w_self_out": noise(streams_of[3], (HD, D), HD ** -0.5, 0.09375, ((0, 4), (1, 8))),
        "w_cross_q": noise(streams_of[4], (D, HD), D ** -0.5, 0.09375, ((0, 8), (1, 4))),
        "w_cross_out": noise(streams_of[5], (HD, D), HD ** -0.5, 0.09375, ((0, 4), (1, 8))),
        "w_ffn_in": noise(streams_of[6], (D, 2, FF), D ** -0.5, 0.09375, ((0, 8), (2, 4))),
        "w_ffn_out": noise(streams_of[7], (FF, D), FF ** -0.5, 0.046875, ((0, 4), (1, 8))),
        "self_keys": noise(streams_of[8], (ROWS, CACHE, HD), 1.0, 6.0, ((0, 32),)),
        "self_values": noise(streams_of[9], (ROWS, CACHE, HD), 1.0, 6.0, ((0, 32),)),
        "cross_keys": noise(streams_of[10], (ROWS, SRC, HD), 1.0, 6.0, ((0, 32),)),
        "cross_values": noise(streams_of[11], (ROWS, SRC, HD), 1.0, 6.0, ((0, 32),)),
        "positions": plant(jax.random.randint(streams_of[12], (ROWS,), 1, CACHE + 1), jax.random.fold_in(streams_of[12], 1), 1, CACHE).astype(jnp.int32),
        "src_len": uneven_parts(streams_of[13], ROWS, ROWS * SRC * 5 // 8, SRC, 1).astype(jnp.int32),
    }


EPSILON = 1e-06

def rounded(values):
    return lax.optimization_barrier(values.astype(jnp.bfloat16)).astype(jnp.float32)

def summed_in(stream, gain_row, weight):
    extra = weight.shape[1:]
    width = D // N_GX
    widened = stream.astype(jnp.float32)
    scaled = rounded(widened * gain_row)
    squares = lax.optimization_barrier(jnp.sum((widened * widened).reshape(ROWS, NEW, N_GX, width), axis=-1))
    squares = lax.optimization_barrier(jnp.sum(rounded(squares), axis=-1))
    pieces = scaled.reshape(ROWS, NEW, N_GX, width)
    weight_parts = weight.reshape((N_GX, width) + extra)

    def accumulate(running, slot_index):
        block = lax.dynamic_index_in_dim(pieces, slot_index, 2, keepdims=False)
        part = lax.dynamic_index_in_dim(weight_parts, slot_index, 0, keepdims=False).astype(jnp.float32)
        return (running + rounded(jnp.tensordot(block, part, axes=1)), None)
    initial = jnp.zeros((ROWS, NEW) + extra, jnp.float32)
    summed, unused = lax.scan(accumulate, initial, jnp.arange(N_GX))
    return (summed, lax.rsqrt(squares / D + EPSILON))

def self_row(items):
    queries, new_keys, new_values, cached_keys, cached_values, position = items
    score_scale = HEAD_DIM ** (-0.5)
    query_f = queries.astype(jnp.float32)
    key_rows = cached_keys.reshape(CACHE, HEADS, HEAD_DIM).astype(jnp.float32)
    value_rows = cached_values.reshape(CACHE, HEADS, HEAD_DIM).astype(jnp.float32)
    scores = jnp.einsum('shd,lhd->hsl', query_f, key_rows) * score_scale
    visible = jnp.arange(CACHE) < position
    cached_exp = jnp.where(visible[None, None, :], jnp.exp(scores), 0.0)
    fresh = jnp.einsum('shd,thd->hst', query_f, new_keys.astype(jnp.float32)) * score_scale
    causal = jnp.arange(NEW)[None, :] <= jnp.arange(NEW)[:, None]
    fresh_exp = jnp.where(causal[None], jnp.exp(fresh), 0.0)
    totals = lax.optimization_barrier(jnp.sum(cached_exp, -1)) + lax.optimization_barrier(jnp.sum(fresh_exp, -1))
    cached_weights = rounded(cached_exp / totals[..., None])
    fresh_weights = rounded(fresh_exp / totals[..., None])
    attended = jnp.einsum('hsl,lhd->shd', cached_weights, value_rows) + jnp.einsum('hst,thd->shd', fresh_weights, new_values.astype(jnp.float32))
    return attended.astype(jnp.bfloat16).reshape(NEW, HD)

def cross_row(items):
    queries, cached_keys, cached_values, length = items
    score_scale = HEAD_DIM ** (-0.5)
    key_rows = cached_keys.reshape(SRC, HEADS, HEAD_DIM).astype(jnp.float32)
    value_rows = cached_values.reshape(SRC, HEADS, HEAD_DIM).astype(jnp.float32)
    scores = jnp.einsum('shd,lhd->hsl', queries.astype(jnp.float32), key_rows) * score_scale
    visible = jnp.arange(SRC) < length
    source_exp = jnp.where(visible[None, None, :], jnp.exp(scores), 0.0)
    totals = lax.optimization_barrier(jnp.sum(source_exp, -1))
    weights = rounded(source_exp / totals[..., None])
    attended = jnp.einsum('hsl,lhd->shd', weights, value_rows)
    return attended.astype(jnp.bfloat16).reshape(NEW, HD)

def reference(tokens, gains, w_qkv, w_self_out, w_cross_q, w_cross_out, w_ffn_in, w_ffn_out, self_keys, self_values, cross_keys, cross_values, positions, src_len):
    summed, factor = summed_in(tokens, gains[0], w_qkv)
    projected = (summed * factor[:, :, None, None]).astype(jnp.bfloat16)
    projected = projected.reshape(ROWS, NEW, 3, HEADS, HEAD_DIM)
    self_mix = lax.map(self_row, (projected[:, :, 0], projected[:, :, 1], projected[:, :, 2], self_keys, self_values, positions))
    self_term = jnp.dot(self_mix.reshape(ROWS * NEW, HD), w_self_out, preferred_element_type=jnp.float32)
    after_self = (tokens.astype(jnp.float32) + self_term.reshape(ROWS, NEW, D)).astype(jnp.bfloat16)
    summed, factor = summed_in(after_self, gains[1], w_cross_q)
    cross_queries = (summed * factor[:, :, None]).astype(jnp.bfloat16).reshape(ROWS, NEW, HEADS, HEAD_DIM)
    cross_mix = lax.map(cross_row, (cross_queries, cross_keys, cross_values, src_len))
    cross_term = jnp.dot(cross_mix.reshape(ROWS * NEW, HD), w_cross_out, preferred_element_type=jnp.float32)
    after_cross = (after_self.astype(jnp.float32) + cross_term.reshape(ROWS, NEW, D)).astype(jnp.bfloat16)
    summed, factor = summed_in(after_cross, gains[2], w_ffn_in)
    gate_up = summed * factor[:, :, None, None]
    hidden = (jax.nn.silu(gate_up[:, :, 0]) * gate_up[:, :, 1]).astype(jnp.bfloat16)
    down_term = jnp.dot(hidden.reshape(ROWS * NEW, FF), w_ffn_out, preferred_element_type=jnp.float32)
    return (after_cross.astype(jnp.float32) + down_term.reshape(ROWS, NEW, D)).astype(jnp.bfloat16)
```

```python
import functools

import jax
import jax.numpy as jnp
from jax import lax
from jax.experimental import pallas as pl
from jax.experimental.pallas import tpu as pltpu
from jax.sharding import PartitionSpec as P

D = 4096
HEAD_DIM = 256
NEW = 2
EPSILON = 1e-06
LANES = 128
MESH = pl.DeviceIdType.MESH
VMEM_LIMIT = 58 * 1024 * 1024


def remote(src, dst, send, recv, device):
    return pltpu.make_async_remote_copy(
        src_ref=src,
        dst_ref=dst,
        send_sem=send,
        recv_sem=recv,
        device_id=device,
        device_id_type=MESH,
    )


def entry_barrier(n, m, i, g):
    barrier = pltpu.get_barrier_semaphore()
    for k in range(1, n):
        pl.semaphore_signal(
            barrier, inc=1, device_id=(lax.rem(i + k, n), g), device_id_type=MESH
        )
    for k in range(1, m):
        pl.semaphore_signal(
            barrier, inc=1, device_id=(i, lax.rem(g + k, m)), device_id_type=MESH
        )
    pl.semaphore_wait(barrier, n + m - 2)


def rows_at(start, size):
    return pl.ds(pl.multiple_of(start * size, size), size)


def project_kernel(
    n, m, blocks, silu,
    x_ref, gain_ref, w_ref, out_ref,
    xg, scaled, part, landed, mine, arrived, total,
    gs, gr, ps, pr, cs, cr, as_, ar,
):
    i, g = lax.axis_index("gx"), lax.axis_index("gy")
    half = n // 2
    c, q = lax.rem(i, 2), i // 2
    other = 1 - c
    partner = q * 2 + other
    here = x_ref.shape[0]
    rows = xg.shape[0] // n
    entry_barrier(n, m, i, g)

    sends = []
    for k in range(1, m):
        copy = remote(
            x_ref, xg.at[rows_at(g, here)], gs.at[k - 1], gr.at[k - 1],
            (i, lax.rem(g + k, m)),
        )
        copy.start()
        sends.append(copy)
    xg[rows_at(g, here), :] = x_ref[...]
    for copy in sends:
        copy.wait_recv()

    gain = gain_ref[...]
    squares = []
    for side in range(2):
        parity = other if side == 0 else c
        sums = []
        for chunk in range(half):
            wide = xg[rows_at(2 * chunk + parity, rows), :].astype(jnp.float32)
            sums.append(jnp.sum(wide * wide, axis=1, keepdims=True))
            scaled[side, pl.ds(chunk * rows, rows), :] = (wide * gain).astype(jnp.bfloat16)
        squares.append(jnp.concatenate(sums, axis=0))

    def block_product(side, block):
        j, start, width, _ = block
        if j < 0:
            return jnp.broadcast_to(squares[side], (half * rows, width))
        return jnp.dot(
            scaled[side], w_ref[j, :, pl.ds(start, width)],
            preferred_element_type=jnp.float32,
        )

    pair = []
    for b, block in enumerate(blocks):
        _, _, width, at = block
        columns = pl.ds(at, width)
        part[:, columns] = block_product(0, block).astype(jnp.bfloat16)
        copy = remote(
            part.at[:, columns], landed.at[:, columns], ps.at[b], pr.at[b], (partner, g)
        )
        copy.start()
        pair.append(copy)

    cross = []
    for b, block in enumerate(blocks):
        _, _, width, at = block
        columns = pl.ds(at, width)
        product = block_product(1, block)
        pair[b].wait_recv()
        mine[:, columns] = (product + landed[:, columns].astype(jnp.float32)).astype(
            jnp.bfloat16
        )
        for k in range(1, half):
            target = lax.rem(q + k, half)
            copy = remote(
                mine.at[rows_at(target, rows), columns], arrived.at[k - 1, :, columns],
                cs.at[k - 1, b], cr.at[k - 1, b], (target * 2 + c, g),
            )
            copy.start()
            cross.append((b, k, copy))

    for b, block in enumerate(blocks):
        _, _, width, at = block
        columns = pl.ds(at, width)
        for bb, k, copy in cross:
            if bb == b:
                copy.wait_recv()
        summed = mine[rows_at(q, rows), columns].astype(jnp.float32)
        for k in range(1, half):
            summed = summed + arrived[k - 1, :, columns].astype(jnp.float32)
        total[:, columns] = summed

    n_columns = blocks[-1][3]
    factor = lax.rsqrt(total[:, pl.ds(n_columns, 1)] / D + EPSILON)
    if silu:
        width = n_columns // 2
        step = min(width, 1024)
        for at in range(0, width, step):
            gate = total[:, pl.ds(at, step)] * factor
            up = total[:, pl.ds(width + at, step)] * factor
            out_ref[:, pl.ds(at, step)] = (
                gate / (1.0 + jnp.exp(-gate)) * up
            ).astype(jnp.bfloat16)
    else:
        piece = rows // m
        scaled_out = mine.at[rows_at(q, rows), pl.ds(0, n_columns)]
        scaled_out[...] = (total[:, pl.ds(0, n_columns)] * factor).astype(jnp.bfloat16)
        away = []
        for k in range(1, m):
            target = lax.rem(g + k, m)
            copy = remote(
                mine.at[
                    pl.ds(pl.multiple_of(q * rows + target * piece, piece), piece),
                    pl.ds(0, n_columns),
                ],
                out_ref.at[g], as_.at[k - 1], ar.at[k - 1], (i, target),
            )
            copy.start()
            away.append(copy)
        out_ref[g] = mine[
            pl.ds(pl.multiple_of(q * rows + g * piece, piece), piece), pl.ds(0, n_columns)
        ]
        for copy in away:
            copy.wait()

    for copy in sends + pair:
        copy.wait_send()
    for _, _, copy in cross:
        copy.wait_send()


def project(n, m, collective_id, silu, x, gain, weight):
    parts, features, width = weight.shape
    here = x.shape[0]
    tokens = here * m
    rows = tokens // n
    half = n // 2
    step = width
    while step > 1024 and step % 2 == 0:
        step //= 2
    if parts == 1 and step == width and width % 512 == 0:
        step = width // 2
    blocks = [
        (j, at, step, j * width + at) for j in range(parts) for at in range(0, width, step)
    ]
    columns = parts * width
    blocks.append((-1, 0, LANES, columns))
    held = columns + LANES
    count = len(blocks)
    if silu:
        out = jax.ShapeDtypeStruct((rows, width), jnp.bfloat16)
    else:
        out = jax.ShapeDtypeStruct((m, rows // m, columns), jnp.bfloat16)
    dma = pltpu.SemaphoreType.DMA
    return pl.pallas_call(
        functools.partial(project_kernel, n, m, tuple(blocks), silu),
        out_shape=out,
        in_specs=[pl.BlockSpec(memory_space=pltpu.VMEM)] * 3,
        out_specs=pl.BlockSpec(memory_space=pltpu.VMEM),
        scratch_shapes=[
            pltpu.VMEM((tokens, features), jnp.bfloat16),
            pltpu.VMEM((2, half * rows, features), jnp.bfloat16),
            pltpu.VMEM((half * rows, held), jnp.bfloat16),
            pltpu.VMEM((half * rows, held), jnp.bfloat16),
            pltpu.VMEM((half * rows, held), jnp.bfloat16),
            pltpu.VMEM((half - 1, rows, held), jnp.bfloat16),
            pltpu.VMEM((rows, held), jnp.float32),
            dma((m - 1,)), dma((m - 1,)),
            dma((count,)), dma((count,)),
            dma((half - 1, count)), dma((half - 1, count)),
            dma((m - 1,)), dma((m - 1,)),
        ],
        compiler_params=pltpu.CompilerParams(
            collective_id=collective_id, has_side_effects=True, vmem_limit_bytes=VMEM_LIMIT
        ),
    )(x, gain, weight)


def output_kernel(
    n, m, regroup,
    a_ref, w_ref, res_ref, out_ref,
    act, part, landed,
    as_, ar, cs, cr, ps, pr, gs, gr,
):
    i, g = lax.axis_index("gx"), lax.axis_index("gy")
    half = n // 2
    c, q = lax.rem(i, 2), i // 2
    partner = q * 2 + 1 - c
    here = res_ref.shape[0]
    rows = act.shape[1]
    entry_barrier(n, m, i, g)

    sends = []
    if regroup:
        piece = rows // m
        away = []
        for k in range(1, m):
            target = lax.rem(g + k, m)
            copy = remote(
                a_ref.at[target], act.at[i, rows_at(g, piece)],
                as_.at[k - 1], ar.at[k - 1], (i, target),
            )
            copy.start()
            away.append(copy)
        act[i, rows_at(g, piece), :] = a_ref[g]
        for copy in away:
            copy.wait_recv()
        sends += away
    else:
        act[i] = a_ref[...]

    cross = []
    for k in range(1, half):
        copy = remote(
            act.at[i], act.at[i], cs.at[k - 1], cr.at[k - 1],
            (lax.rem(q + k, half) * 2 + c, g),
        )
        copy.start()
        cross.append(copy)
    pair = []
    for k in range(half):
        chip = lax.rem(q + half - k, half)
        source = chip * 2 + c
        if k > 0:
            cross[k - 1].wait_recv()
        copy = remote(act.at[source], act.at[source], ps.at[k], pr.at[k], (partner, g))
        copy.start()
        pair.append(copy)
        if k > 0:
            multiply(act, w_ref, part, pair[k - 1], lax.rem(q + half - (k - 1), half), rows)
    multiply(act, w_ref, part, pair[half - 1], lax.rem(q + 1, half), rows)

    summed = []
    for k in range(1, m):
        target = lax.rem(g + k, m)
        copy = remote(
            part.at[rows_at(target, here)], landed.at[k - 1],
            gs.at[k - 1], gr.at[k - 1], (i, target),
        )
        copy.start()
        summed.append(copy)
    result = part[rows_at(g, here), :].astype(jnp.float32)
    for k in range(1, m):
        summed[k - 1].wait_recv()
        result = result + landed[k - 1].astype(jnp.float32)
    out_ref[...] = (res_ref[...].astype(jnp.float32) + result).astype(jnp.bfloat16)
    for copy in sends + cross + pair + summed:
        copy.wait_send()


def multiply(act, w_ref, part, copy, chip, rows):
    copy.wait_recv()
    block = act[pl.ds(chip * 2, 2)].reshape(2 * rows, act.shape[2])
    part[rows_at(chip, 2 * rows), :] = jnp.dot(
        block, w_ref[...], preferred_element_type=jnp.float32
    ).astype(jnp.bfloat16)


def output(n, m, collective_id, regroup, activity, weight, residual):
    here, features = residual.shape
    tokens = here * m
    rows = tokens // n
    half = n // 2
    dma = pltpu.SemaphoreType.DMA
    return pl.pallas_call(
        functools.partial(output_kernel, n, m, regroup),
        out_shape=jax.ShapeDtypeStruct((here, features), jnp.bfloat16),
        in_specs=[pl.BlockSpec(memory_space=pltpu.VMEM)] * 3,
        out_specs=pl.BlockSpec(memory_space=pltpu.VMEM),
        scratch_shapes=[
            pltpu.VMEM((n, rows, weight.shape[0]), jnp.bfloat16),
            pltpu.VMEM((tokens, features), jnp.bfloat16),
            pltpu.VMEM((m - 1, here, features), jnp.bfloat16),
            dma((m - 1,)), dma((m - 1,)),
            dma((half - 1,)), dma((half - 1,)),
            dma((half,)), dma((half,)),
            dma((m - 1,)), dma((m - 1,)),
        ],
        compiler_params=pltpu.CompilerParams(
            collective_id=collective_id, has_side_effects=True, vmem_limit_bytes=VMEM_LIMIT
        ),
    )(activity, weight, residual)


def contract(left, right):
    return lax.dot_general(
        left, right, (((1,), (1,)), ((), ())), preferred_element_type=jnp.float32
    )


def attend_kernel(heads, own, q_ref, k_ref, v_ref, length_ref, out_ref):
    rows, slots, _ = k_ref.shape
    count = q_ref.shape[1]
    scale = HEAD_DIM ** (-0.5)
    shape = (count, rows * slots)
    row = lax.broadcasted_iota(jnp.int32, shape, 0) // NEW
    column = lax.broadcasted_iota(jnp.int32, shape, 1)
    slot = column - row * slots
    visible = (slot >= 0) & (slot < length_ref[...])
    if own:
        mine = (count, count)
        token = lax.broadcasted_iota(jnp.int32, mine, 0)
        key = lax.broadcasted_iota(jnp.int32, mine, 1)
        causal = (token // NEW == key // NEW) & (key <= token)
    for h in range(heads):
        span = pl.ds(h * HEAD_DIM, HEAD_DIM)
        query = q_ref[0, :, span]
        keys = k_ref[:, :, span].reshape(rows * slots, HEAD_DIM)
        values = v_ref[:, :, span].reshape(rows * slots, HEAD_DIM)
        exps = jnp.where(visible, jnp.exp(contract(query, keys) * scale), 0.0)
        totals = jnp.sum(exps, axis=1, keepdims=True)
        if own:
            new_keys = q_ref[0, :, pl.ds((heads + h) * HEAD_DIM, HEAD_DIM)]
            new_values = q_ref[0, :, pl.ds((2 * heads + h) * HEAD_DIM, HEAD_DIM)]
            fresh = jnp.where(causal, jnp.exp(contract(query, new_keys) * scale), 0.0)
            totals = totals + jnp.sum(fresh, axis=1, keepdims=True)
        mix = jnp.dot(
            (exps / totals).astype(jnp.bfloat16), values, preferred_element_type=jnp.float32
        )
        if own:
            mix = mix + jnp.dot(
                (fresh / totals).astype(jnp.bfloat16), new_values,
                preferred_element_type=jnp.float32,
            )
        out_ref[0, :, span] = mix.astype(jnp.bfloat16)


def attend(own, queries, keys, values, lengths):
    m, count, columns = queries.shape
    rows, slots, features = keys.shape
    width = features // m
    spread = jnp.repeat(lengths, count // rows).reshape(count, 1)
    return pl.pallas_call(
        functools.partial(attend_kernel, width // HEAD_DIM, own),
        out_shape=jax.ShapeDtypeStruct((m, count, width), jnp.bfloat16),
        grid=(m,),
        in_specs=[
            pl.BlockSpec((1, count, columns), lambda s: (s, 0, 0)),
            pl.BlockSpec((rows, slots, width), lambda s: (0, 0, s)),
            pl.BlockSpec((rows, slots, width), lambda s: (0, 0, s)),
            pl.BlockSpec((count, 1), lambda s: (0, 0)),
        ],
        out_specs=pl.BlockSpec((1, count, width), lambda s: (s, 0, 0)),
        compiler_params=pltpu.CompilerParams(vmem_limit_bytes=VMEM_LIMIT),
    )(queries, keys, values, spread)


def per_device(
    tokens,
    gains,
    w_qkv,
    w_self_out,
    w_cross_q,
    w_cross_out,
    w_ffn_in,
    w_ffn_out,
    self_keys,
    self_values,
    cross_keys,
    cross_values,
    positions,
    src_len,
):
    n, m = lax.axis_size("gx"), lax.axis_size("gy")
    stream = tokens.reshape(tokens.shape[0] * NEW, tokens.shape[2])
    projected = project(n, m, 0, False, stream, gains[0:1], jnp.transpose(w_qkv, (1, 0, 2)))
    mixed = attend(True, projected, self_keys, self_values, positions)
    after_self = output(n, m, 1, True, mixed, w_self_out, stream)
    queries = project(n, m, 2, False, after_self, gains[1:2], w_cross_q[None])
    crossed = attend(False, queries, cross_keys, cross_values, src_len)
    after_cross = output(n, m, 3, True, crossed, w_cross_out, after_self)
    hidden = project(
        n, m, 4, True, after_cross, gains[2:3], jnp.transpose(w_ffn_in, (1, 0, 2))
    )
    result = output(n, m, 5, False, hidden, w_ffn_out, after_cross)
    return result.reshape(tokens.shape)


def solution(mesh):
    return jax.shard_map(
        per_device,
        mesh=mesh,
        in_specs=(
            P("gy", None, "gx"),
            P(None, "gx"),
            P("gx", None, "gy"),
            P("gy", "gx"),
            P("gx", "gy"),
            P("gy", "gx"),
            P("gx", None, "gy"),
            P("gy", "gx"),
            P(("gx", "gy"), None, None),
            P(("gx", "gy"), None, None),
            P(("gx", "gy"), None, None),
            P(("gx", "gy"), None, None),
            P(("gx", "gy")),
            P(("gx", "gy")),
        ),
        out_specs=P("gy", None, "gx"),
        check_vma=False,
    )
```

```python
import functools

import jax
import jax.numpy as jnp
from jax import lax
from jax.experimental import pallas as pl
from jax.experimental.pallas import tpu as pltpu
from jax.sharding import PartitionSpec as P

D = 4096
HEAD_DIM = 256
NEW = 2
EPSILON = 1e-06
LANES = 128
MESH = pl.DeviceIdType.MESH
VMEM_LIMIT = 58 * 1024 * 1024


def remote(src, dst, send, recv, device):
    return pltpu.make_async_remote_copy(
        src_ref=src,
        dst_ref=dst,
        send_sem=send,
        recv_sem=recv,
        device_id=device,
        device_id_type=MESH,
    )


def entry_barrier(n, m, i, g):
    barrier = pltpu.get_barrier_semaphore()
    for k in range(1, n):
        pl.semaphore_signal(
            barrier, inc=1, device_id=(lax.rem(i + k, n), g), device_id_type=MESH
        )
    for k in range(1, m):
        pl.semaphore_signal(
            barrier, inc=1, device_id=(i, lax.rem(g + k, m)), device_id_type=MESH
        )
    pl.semaphore_wait(barrier, n + m - 2)


def rows_at(start, size):
    return pl.ds(pl.multiple_of(start * size, size), size)


def project_kernel(
    n, m, blocks, silu,
    x_ref, gain_ref, w_ref, out_ref,
    xg, scaled, part, landed, mine, arrived, total,
    held_w, gs, gr, ps, pr, cs, cr, as_, ar, ws,
):
    i, g = lax.axis_index("gx"), lax.axis_index("gy")
    half = n // 2
    c, q = lax.rem(i, 2), i // 2
    other = 1 - c
    partner = q * 2 + other
    here = x_ref.shape[0]
    rows = xg.shape[0] // n
    loads = [
        pltpu.make_async_copy(w_ref.at[j], held_w.at[j], ws.at[j])
        for j in range(w_ref.shape[0])
    ]
    for load in loads:
        load.start()
    entry_barrier(n, m, i, g)

    sends = []
    for k in range(1, m):
        copy = remote(
            x_ref, xg.at[rows_at(g, here)], gs.at[k - 1], gr.at[k - 1],
            (i, lax.rem(g + k, m)),
        )
        copy.start()
        sends.append(copy)
    xg[rows_at(g, here), :] = x_ref[...]
    for copy in sends:
        copy.wait_recv()

    gain = gain_ref[...]
    squares = []
    for side in range(2):
        parity = other if side == 0 else c
        sums = []
        for chunk in range(half):
            wide = xg[rows_at(2 * chunk + parity, rows), :].astype(jnp.float32)
            sums.append(jnp.sum(wide * wide, axis=1, keepdims=True))
            scaled[side, pl.ds(chunk * rows, rows), :] = (wide * gain).astype(jnp.bfloat16)
        squares.append(jnp.concatenate(sums, axis=0))

    def block_product(side, block):
        j, start, width, _ = block
        if j < 0:
            return jnp.broadcast_to(squares[side], (half * rows, width))
        return jnp.dot(
            scaled[side], held_w[j, :, pl.ds(start, width)],
            preferred_element_type=jnp.float32,
        )

    for load in loads:
        load.wait()
    pair = []
    for b, block in enumerate(blocks):
        _, _, width, at = block
        columns = pl.ds(at, width)
        part[:, columns] = block_product(0, block).astype(jnp.bfloat16)
        copy = remote(
            part.at[:, columns], landed.at[:, columns], ps.at[b], pr.at[b], (partner, g)
        )
        copy.start()
        pair.append(copy)

    cross = []
    for b, block in enumerate(blocks):
        _, _, width, at = block
        columns = pl.ds(at, width)
        product = block_product(1, block)
        pair[b].wait_recv()
        mine[:, columns] = (product + landed[:, columns].astype(jnp.float32)).astype(
            jnp.bfloat16
        )
        for k in range(1, half):
            target = lax.rem(q + k, half)
            copy = remote(
                mine.at[rows_at(target, rows), columns], arrived.at[k - 1, :, columns],
                cs.at[k - 1, b], cr.at[k - 1, b], (target * 2 + c, g),
            )
            copy.start()
            cross.append((b, k, copy))

    n_columns = blocks[0][3]
    piece = rows // m
    away = []
    for b, block in enumerate(blocks):
        _, _, width, at = block
        columns = pl.ds(at, width)
        for bb, k, copy in cross:
            if bb == b:
                copy.wait_recv()
        summed = mine[rows_at(q, rows), columns].astype(jnp.float32)
        for k in range(1, half):
            summed = summed + arrived[k - 1, :, columns].astype(jnp.float32)
        if b == 0:
            factor = lax.rsqrt(summed[:, 0:1] / D + EPSILON)
        elif silu:
            total[:, columns] = summed * factor
        else:
            mine[rows_at(q, rows), columns] = (summed * factor).astype(jnp.bfloat16)
            for k in range(1, m):
                target = lax.rem(g + k, m)
                copy = remote(
                    mine.at[
                        pl.ds(pl.multiple_of(q * rows + target * piece, piece), piece),
                        columns,
                    ],
                    out_ref.at[g, :, columns], as_.at[k - 1, b], ar.at[k - 1, b],
                    (i, target),
                )
                copy.start()
                away.append(copy)
            out_ref[g, :, columns] = mine[
                pl.ds(pl.multiple_of(q * rows + g * piece, piece), piece), columns
            ]
    if silu:
        width = n_columns // 2
        step = min(width, 1024)
        for at in range(0, width, step):
            gate = total[:, pl.ds(at, step)]
            up = total[:, pl.ds(width + at, step)]
            out_ref[:, pl.ds(at, step)] = (
                gate / (1.0 + jnp.exp(-gate)) * up
            ).astype(jnp.bfloat16)
    for copy in away:
        copy.wait()

    for copy in sends + pair:
        copy.wait_send()
    for _, _, copy in cross:
        copy.wait_send()


def project(n, m, collective_id, silu, x, gain, weight):
    parts, features, width = weight.shape
    here = x.shape[0]
    tokens = here * m
    rows = tokens // n
    half = n // 2
    step = width
    while step > 1024 and step % 2 == 0:
        step //= 2
    if parts == 1 and step == width and width % 512 == 0:
        step = width // 2
    blocks = [
        (j, at, step, j * width + at) for j in range(parts) for at in range(0, width, step)
    ]
    columns = parts * width
    blocks.insert(0, (-1, 0, LANES, columns))
    held = columns + LANES
    count = len(blocks)
    if silu:
        out = jax.ShapeDtypeStruct((rows, width), jnp.bfloat16)
    else:
        out = jax.ShapeDtypeStruct((m, rows // m, columns), jnp.bfloat16)
    dma = pltpu.SemaphoreType.DMA
    return pl.pallas_call(
        functools.partial(project_kernel, n, m, tuple(blocks), silu),
        out_shape=out,
        in_specs=[
            pl.BlockSpec(memory_space=pltpu.VMEM),
            pl.BlockSpec(memory_space=pltpu.VMEM),
            pl.BlockSpec(memory_space=pl.ANY),
        ],
        out_specs=pl.BlockSpec(memory_space=pltpu.VMEM),
        scratch_shapes=[
            pltpu.VMEM((tokens, features), jnp.bfloat16),
            pltpu.VMEM((2, half * rows, features), jnp.bfloat16),
            pltpu.VMEM((half * rows, held), jnp.bfloat16),
            pltpu.VMEM((half * rows, held), jnp.bfloat16),
            pltpu.VMEM((half * rows, held), jnp.bfloat16),
            pltpu.VMEM((half - 1, rows, held), jnp.bfloat16),
            pltpu.VMEM((rows, held), jnp.float32),
            pltpu.VMEM(weight.shape, jnp.bfloat16),
            dma((m - 1,)), dma((m - 1,)),
            dma((count,)), dma((count,)),
            dma((half - 1, count)), dma((half - 1, count)),
            dma((m - 1, count)), dma((m - 1, count)),
            dma((parts,)),
        ],
        compiler_params=pltpu.CompilerParams(
            collective_id=collective_id, has_side_effects=True, vmem_limit_bytes=VMEM_LIMIT
        ),
    )(x, gain, weight)


def output_kernel(
    n, m, regroup,
    a_ref, w_ref, res_ref, out_ref,
    act, part, landed, held_w,
    as_, ar, cs, cr, ps, pr, gs, gr, ws,
):
    i, g = lax.axis_index("gx"), lax.axis_index("gy")
    half = n // 2
    c, q = lax.rem(i, 2), i // 2
    partner = q * 2 + 1 - c
    here = res_ref.shape[0]
    rows = act.shape[1]
    load = pltpu.make_async_copy(w_ref, held_w, ws.at[0])
    load.start()
    entry_barrier(n, m, i, g)

    sends = []
    if regroup:
        piece = rows // m
        away = []
        for k in range(1, m):
            target = lax.rem(g + k, m)
            copy = remote(
                a_ref.at[target], act.at[i, rows_at(g, piece)],
                as_.at[k - 1], ar.at[k - 1], (i, target),
            )
            copy.start()
            away.append(copy)
        act[i, rows_at(g, piece), :] = a_ref[g]
        for copy in away:
            copy.wait_recv()
        sends += away
    else:
        act[i] = a_ref[...]

    cross = []
    for k in range(1, half):
        copy = remote(
            act.at[i], act.at[i], cs.at[k - 1], cr.at[k - 1],
            (lax.rem(q + k, half) * 2 + c, g),
        )
        copy.start()
        cross.append(copy)
    early = half == m and 2 * rows == here
    summed = []
    for k in range(1, m):
        target = lax.rem(g + k, m)
        summed.append(
            remote(
                part.at[rows_at(target, here)], landed.at[k - 1],
                gs.at[k - 1], gr.at[k - 1], (i, target),
            )
        )

    def finish(k):
        chip = lax.rem(q + half - k, half)
        multiply(act, held_w, part, pair[k], chip, rows)
        if early:
            ahead = lax.rem(chip + m - g, m)

            @pl.when(ahead != 0)
            def _():
                remote(
                    part.at[rows_at(chip, here)], landed.at[ahead - 1],
                    gs.at[ahead - 1], gr.at[ahead - 1], (i, chip),
                ).start()

    pair = []
    for k in range(half):
        chip = lax.rem(q + half - k, half)
        source = chip * 2 + c
        if k > 0:
            cross[k - 1].wait_recv()
        copy = remote(act.at[source], act.at[source], ps.at[k], pr.at[k], (partner, g))
        copy.start()
        pair.append(copy)
        if k == 0:
            load.wait()
        else:
            finish(k - 1)
    finish(half - 1)
    if not early:
        for copy in summed:
            copy.start()
    result = part[rows_at(g, here), :].astype(jnp.float32)
    for k in range(1, m):
        summed[k - 1].wait_recv()
        result = result + landed[k - 1].astype(jnp.float32)
    out_ref[...] = (res_ref[...].astype(jnp.float32) + result).astype(jnp.bfloat16)
    for copy in sends + cross + pair + summed:
        copy.wait_send()


def multiply(act, w_ref, part, copy, chip, rows):
    copy.wait_recv()
    block = act[pl.ds(chip * 2, 2)].reshape(2 * rows, act.shape[2])
    part[rows_at(chip, 2 * rows), :] = jnp.dot(
        block, w_ref[...], preferred_element_type=jnp.float32
    ).astype(jnp.bfloat16)


def output(n, m, collective_id, regroup, activity, weight, residual):
    here, features = residual.shape
    tokens = here * m
    rows = tokens // n
    half = n // 2
    dma = pltpu.SemaphoreType.DMA
    return pl.pallas_call(
        functools.partial(output_kernel, n, m, regroup),
        out_shape=jax.ShapeDtypeStruct((here, features), jnp.bfloat16),
        in_specs=[
            pl.BlockSpec(memory_space=pltpu.VMEM),
            pl.BlockSpec(memory_space=pl.ANY),
            pl.BlockSpec(memory_space=pltpu.VMEM),
        ],
        out_specs=pl.BlockSpec(memory_space=pltpu.VMEM),
        scratch_shapes=[
            pltpu.VMEM((n, rows, weight.shape[0]), jnp.bfloat16),
            pltpu.VMEM((tokens, features), jnp.bfloat16),
            pltpu.VMEM((m - 1, here, features), jnp.bfloat16),
            pltpu.VMEM(weight.shape, jnp.bfloat16),
            dma((m - 1,)), dma((m - 1,)),
            dma((half - 1,)), dma((half - 1,)),
            dma((half,)), dma((half,)),
            dma((m - 1,)), dma((m - 1,)),
            dma((1,)),
        ],
        compiler_params=pltpu.CompilerParams(
            collective_id=collective_id, has_side_effects=True, vmem_limit_bytes=VMEM_LIMIT
        ),
    )(activity, weight, residual)


def contract(left, right):
    return lax.dot_general(
        left, right, (((1,), (1,)), ((), ())), preferred_element_type=jnp.float32
    )


def attend_kernel(heads, own, q_ref, k_ref, v_ref, length_ref, out_ref):
    rows, slots, _ = k_ref.shape
    count = q_ref.shape[1]
    scale = HEAD_DIM ** (-0.5)
    shape = (count, rows * slots)
    row = lax.broadcasted_iota(jnp.int32, shape, 0) // NEW
    column = lax.broadcasted_iota(jnp.int32, shape, 1)
    slot = column - row * slots
    visible = (slot >= 0) & (slot < length_ref[...])
    if own:
        mine = (count, count)
        token = lax.broadcasted_iota(jnp.int32, mine, 0)
        key = lax.broadcasted_iota(jnp.int32, mine, 1)
        causal = (token // NEW == key // NEW) & (key <= token)
    for h in range(heads):
        span = pl.ds(h * HEAD_DIM, HEAD_DIM)
        query = q_ref[0, :, span]
        keys = k_ref[:, :, span].reshape(rows * slots, HEAD_DIM)
        values = v_ref[:, :, span].reshape(rows * slots, HEAD_DIM)
        exps = jnp.where(visible, jnp.exp(contract(query, keys) * scale), 0.0)
        totals = jnp.sum(exps, axis=1, keepdims=True)
        if own:
            new_keys = q_ref[0, :, pl.ds((heads + h) * HEAD_DIM, HEAD_DIM)]
            new_values = q_ref[0, :, pl.ds((2 * heads + h) * HEAD_DIM, HEAD_DIM)]
            fresh = jnp.where(causal, jnp.exp(contract(query, new_keys) * scale), 0.0)
            totals = totals + jnp.sum(fresh, axis=1, keepdims=True)
        mix = jnp.dot(
            (exps / totals).astype(jnp.bfloat16), values, preferred_element_type=jnp.float32
        )
        if own:
            mix = mix + jnp.dot(
                (fresh / totals).astype(jnp.bfloat16), new_values,
                preferred_element_type=jnp.float32,
            )
        out_ref[0, :, span] = mix.astype(jnp.bfloat16)


def attend(own, queries, keys, values, lengths):
    m, count, columns = queries.shape
    rows, slots, features = keys.shape
    width = features // m
    spread = jnp.repeat(lengths, count // rows).reshape(count, 1)
    return pl.pallas_call(
        functools.partial(attend_kernel, width // HEAD_DIM, own),
        out_shape=jax.ShapeDtypeStruct((m, count, width), jnp.bfloat16),
        grid=(m,),
        in_specs=[
            pl.BlockSpec((1, count, columns), lambda s: (s, 0, 0)),
            pl.BlockSpec((rows, slots, width), lambda s: (0, 0, s)),
            pl.BlockSpec((rows, slots, width), lambda s: (0, 0, s)),
            pl.BlockSpec((count, 1), lambda s: (0, 0)),
        ],
        out_specs=pl.BlockSpec((1, count, width), lambda s: (s, 0, 0)),
        compiler_params=pltpu.CompilerParams(vmem_limit_bytes=VMEM_LIMIT),
    )(queries, keys, values, spread)


def per_device(
    tokens,
    gains,
    w_qkv,
    w_self_out,
    w_cross_q,
    w_cross_out,
    w_ffn_in,
    w_ffn_out,
    self_keys,
    self_values,
    cross_keys,
    cross_values,
    positions,
    src_len,
):
    n, m = lax.axis_size("gx"), lax.axis_size("gy")
    stream = tokens.reshape(tokens.shape[0] * NEW, tokens.shape[2])
    projected = project(n, m, 0, False, stream, gains[0:1], jnp.transpose(w_qkv, (1, 0, 2)))
    mixed = attend(True, projected, self_keys, self_values, positions)
    after_self = output(n, m, 1, True, mixed, w_self_out, stream)
    queries = project(n, m, 2, False, after_self, gains[1:2], w_cross_q[None])
    crossed = attend(False, queries, cross_keys, cross_values, src_len)
    after_cross = output(n, m, 3, True, crossed, w_cross_out, after_self)
    hidden = project(
        n, m, 4, True, after_cross, gains[2:3], jnp.transpose(w_ffn_in, (1, 0, 2))
    )
    result = output(n, m, 5, False, hidden, w_ffn_out, after_cross)
    return result.reshape(tokens.shape)


def solution(mesh):
    return jax.shard_map(
        per_device,
        mesh=mesh,
        in_specs=(
            P("gy", None, "gx"),
            P(None, "gx"),
            P("gx", None, "gy"),
            P("gy", "gx"),
            P("gx", "gy"),
            P("gy", "gx"),
            P("gx", None, "gy"),
            P("gy", "gx"),
            P(("gx", "gy"), None, None),
            P(("gx", "gy"), None, None),
            P(("gx", "gy"), None, None),
            P(("gx", "gy"), None, None),
            P(("gx", "gy")),
            P(("gx", "gy")),
        ),
        out_specs=P("gy", None, "gx"),
        check_vma=False,
    )
```

```python
import functools

import jax
import jax.numpy as jnp
from jax import lax
from jax.experimental import pallas as pl
from jax.experimental.pallas import tpu as pltpu
from jax.sharding import PartitionSpec as P

D = 4096
HEAD_DIM = 256
NEW = 2
EPSILON = 1e-06
LANES = 128
MESH = pl.DeviceIdType.MESH
VMEM_LIMIT = 58 * 1024 * 1024


def remote(src, dst, send, recv, device):
    return pltpu.make_async_remote_copy(
        src_ref=src,
        dst_ref=dst,
        send_sem=send,
        recv_sem=recv,
        device_id=device,
        device_id_type=MESH,
    )


def entry_barrier(n, m, i, g):
    barrier = pltpu.get_barrier_semaphore()
    for k in range(1, n):
        pl.semaphore_signal(
            barrier, inc=1, device_id=(lax.rem(i + k, n), g), device_id_type=MESH
        )
    for k in range(1, m):
        pl.semaphore_signal(
            barrier, inc=1, device_id=(i, lax.rem(g + k, m)), device_id_type=MESH
        )
    pl.semaphore_wait(barrier, n + m - 2)


def rows_at(start, size):
    return pl.ds(pl.multiple_of(start * size, size), size)


def project_kernel(
    n, m, blocks, silu,
    x_ref, gain_ref, w_ref, out_ref,
    xg, scaled, part, landed, mine, arrived, total,
    held_w, gs, gr, ps, pr, cs, cr, as_, ar, ws,
):
    i, g = lax.axis_index("gx"), lax.axis_index("gy")
    half = n // 2
    c, q = lax.rem(i, 2), i // 2
    other = 1 - c
    partner = q * 2 + other
    here = x_ref.shape[0]
    rows = xg.shape[0] // n
    loads = [
        pltpu.make_async_copy(w_ref.at[j], held_w.at[j], ws.at[j])
        for j in range(w_ref.shape[0])
    ]
    for load in loads:
        load.start()
    entry_barrier(n, m, i, g)

    sends = []
    for k in range(1, m):
        copy = remote(
            x_ref, xg.at[rows_at(g, here)], gs.at[k - 1], gr.at[k - 1],
            (i, lax.rem(g + k, m)),
        )
        copy.start()
        sends.append(copy)
    xg[rows_at(g, here), :] = x_ref[...]
    for copy in sends:
        copy.wait_recv()

    gain = gain_ref[...]
    squares = []
    for side in range(2):
        parity = other if side == 0 else c
        sums = []
        for chunk in range(half):
            wide = xg[rows_at(2 * chunk + parity, rows), :].astype(jnp.float32)
            sums.append(jnp.sum(wide * wide, axis=1, keepdims=True))
            scaled[side, pl.ds(chunk * rows, rows), :] = (wide * gain).astype(jnp.bfloat16)
        squares.append(jnp.concatenate(sums, axis=0))

    def block_product(side, block):
        j, start, width, _ = block
        if j < 0:
            return jnp.broadcast_to(squares[side], (half * rows, width))
        return jnp.dot(
            scaled[side], held_w[j, :, pl.ds(start, width)],
            preferred_element_type=jnp.float32,
        )

    for load in loads:
        load.wait()
    pair = []
    for b, block in enumerate(blocks):
        _, _, width, at = block
        columns = pl.ds(at, width)
        part[:, columns] = block_product(0, block).astype(jnp.bfloat16)
        copy = remote(
            part.at[:, columns], landed.at[:, columns], ps.at[b], pr.at[b], (partner, g)
        )
        copy.start()
        pair.append(copy)

    two_step = half == 4
    beside = q + 1 - 2 * lax.rem(q, 2)
    across = lax.rem(q + 2, 4)

    def legs(b):
        near, far = (beside, across) if b % 2 == 0 else (across, beside)
        return ((near, near), (3 - q, near), (far, far))

    def leg_copy(b, k, columns):
        chunk, chip = legs(b)[k]
        return remote(
            mine.at[rows_at(chunk, rows), columns], arrived.at[k, :, columns],
            cs.at[k, b], cr.at[k, b], (chip * 2 + c, g),
        )

    cross = []
    for b, block in enumerate(blocks):
        _, _, width, at = block
        columns = pl.ds(at, width)
        product = block_product(1, block)
        pair[b].wait_recv()
        mine[:, columns] = (product + landed[:, columns].astype(jnp.float32)).astype(
            jnp.bfloat16
        )
        if two_step:
            for k in range(2):
                copy = leg_copy(b, k, columns)
                copy.start()
                cross.append((b, k, copy))
            continue
        for k in range(1, half):
            target = lax.rem(q + k, half)
            copy = remote(
                mine.at[rows_at(target, rows), columns], arrived.at[k - 1, :, columns],
                cs.at[k - 1, b], cr.at[k - 1, b], (target * 2 + c, g),
            )
            copy.start()
            cross.append((b, k, copy))

    if two_step:
        for b, block in enumerate(blocks):
            _, _, width, at = block
            columns = pl.ds(at, width)
            for copy in (cross[2 * b][2], cross[2 * b + 1][2]):
                copy.wait_recv()
            onward = rows_at(legs(b)[2][0], rows)
            mine[onward, columns] = (
                mine[onward, columns].astype(jnp.float32)
                + arrived[1, :, columns].astype(jnp.float32)
            ).astype(jnp.bfloat16)
            copy = leg_copy(b, 2, columns)
            copy.start()
            cross.append((b, 2, copy))

    n_columns = blocks[0][3]
    piece = rows // m
    away = []
    for b, block in enumerate(blocks):
        _, _, width, at = block
        columns = pl.ds(at, width)
        for bb, k, copy in cross:
            if bb == b and (k == 2 or not two_step):
                copy.wait_recv()
        summed = mine[rows_at(q, rows), columns].astype(jnp.float32)
        for k in (0, 2) if two_step else range(half - 1):
            summed = summed + arrived[k, :, columns].astype(jnp.float32)
        if b == 0:
            factor = lax.rsqrt(summed[:, 0:1] / D + EPSILON)
        elif silu:
            total[:, columns] = summed * factor
        else:
            mine[rows_at(q, rows), columns] = (summed * factor).astype(jnp.bfloat16)
            for k in range(1, m):
                target = lax.rem(g + k, m)
                copy = remote(
                    mine.at[
                        pl.ds(pl.multiple_of(q * rows + target * piece, piece), piece),
                        columns,
                    ],
                    out_ref.at[g, :, columns], as_.at[k - 1, b], ar.at[k - 1, b],
                    (i, target),
                )
                copy.start()
                away.append(copy)
            out_ref[g, :, columns] = mine[
                pl.ds(pl.multiple_of(q * rows + g * piece, piece), piece), columns
            ]
    if silu:
        width = n_columns // 2
        step = min(width, 1024)
        for at in range(0, width, step):
            gate = total[:, pl.ds(at, step)]
            up = total[:, pl.ds(width + at, step)]
            out_ref[:, pl.ds(at, step)] = (
                gate / (1.0 + jnp.exp(-gate)) * up
            ).astype(jnp.bfloat16)
    for copy in away:
        copy.wait()

    for copy in sends + pair:
        copy.wait_send()
    for _, _, copy in cross:
        copy.wait_send()


def project(n, m, collective_id, silu, x, gain, weight):
    parts, features, width = weight.shape
    here = x.shape[0]
    tokens = here * m
    rows = tokens // n
    half = n // 2
    step = width
    while step > 1024 and step % 2 == 0:
        step //= 2
    if (parts * (width // step)) % 2 == 1 and step % 256 == 0:
        step //= 2
    blocks = [
        (j, at, step, j * width + at) for j in range(parts) for at in range(0, width, step)
    ]
    columns = parts * width
    blocks.insert(0, (-1, 0, LANES, columns))
    held = columns + LANES
    count = len(blocks)
    if silu:
        out = jax.ShapeDtypeStruct((rows, width), jnp.bfloat16)
    else:
        out = jax.ShapeDtypeStruct((m, rows // m, columns), jnp.bfloat16)
    dma = pltpu.SemaphoreType.DMA
    return pl.pallas_call(
        functools.partial(project_kernel, n, m, tuple(blocks), silu),
        out_shape=out,
        in_specs=[
            pl.BlockSpec(memory_space=pltpu.VMEM),
            pl.BlockSpec(memory_space=pltpu.VMEM),
            pl.BlockSpec(memory_space=pl.ANY),
        ],
        out_specs=pl.BlockSpec(memory_space=pltpu.VMEM),
        scratch_shapes=[
            pltpu.VMEM((tokens, features), jnp.bfloat16),
            pltpu.VMEM((2, half * rows, features), jnp.bfloat16),
            pltpu.VMEM((half * rows, held), jnp.bfloat16),
            pltpu.VMEM((half * rows, held), jnp.bfloat16),
            pltpu.VMEM((half * rows, held), jnp.bfloat16),
            pltpu.VMEM((half - 1, rows, held), jnp.bfloat16),
            pltpu.VMEM((rows, held), jnp.float32),
            pltpu.VMEM(weight.shape, jnp.bfloat16),
            dma((m - 1,)), dma((m - 1,)),
            dma((count,)), dma((count,)),
            dma((half - 1, count)), dma((half - 1, count)),
            dma((m - 1, count)), dma((m - 1, count)),
            dma((parts,)),
        ],
        compiler_params=pltpu.CompilerParams(
            collective_id=collective_id, has_side_effects=True, vmem_limit_bytes=VMEM_LIMIT
        ),
    )(x, gain, weight)


def output_kernel(
    n, m, regroup,
    a_ref, w_ref, res_ref, out_ref,
    act, part, landed, held_w,
    as_, ar, cs, cr, ps, pr, gs, gr, ws,
):
    i, g = lax.axis_index("gx"), lax.axis_index("gy")
    half = n // 2
    c, q = lax.rem(i, 2), i // 2
    partner = q * 2 + 1 - c
    here = res_ref.shape[0]
    rows = act.shape[1]
    load = pltpu.make_async_copy(w_ref, held_w, ws.at[0])
    load.start()
    entry_barrier(n, m, i, g)

    sends = []
    if regroup:
        piece = rows // m
        away = []
        for k in range(1, m):
            target = lax.rem(g + k, m)
            copy = remote(
                a_ref.at[target], act.at[i, rows_at(g, piece)],
                as_.at[k - 1], ar.at[k - 1], (i, target),
            )
            copy.start()
            away.append(copy)
        act[i, rows_at(g, piece), :] = a_ref[g]
        for copy in away:
            copy.wait_recv()
        sends += away
    else:
        act[i] = a_ref[...]

    cross = []
    for k in range(1, half):
        copy = remote(
            act.at[i], act.at[i], cs.at[k - 1], cr.at[k - 1],
            (lax.rem(q + k, half) * 2 + c, g),
        )
        copy.start()
        cross.append(copy)
    early = half == m and 2 * rows == here
    summed = []
    for k in range(1, m):
        target = lax.rem(g + k, m)
        summed.append(
            remote(
                part.at[rows_at(target, here)], landed.at[k - 1],
                gs.at[k - 1], gr.at[k - 1], (i, target),
            )
        )

    def finish(k):
        chip = lax.rem(q + half - k, half)
        multiply(act, held_w, part, pair[k], chip, rows)
        if early:
            ahead = lax.rem(chip + m - g, m)

            @pl.when(ahead != 0)
            def _():
                remote(
                    part.at[rows_at(chip, here)], landed.at[ahead - 1],
                    gs.at[ahead - 1], gr.at[ahead - 1], (i, chip),
                ).start()

    pair = []
    for k in range(half):
        chip = lax.rem(q + half - k, half)
        source = chip * 2 + c
        if k > 0:
            cross[k - 1].wait_recv()
        copy = remote(act.at[source], act.at[source], ps.at[k], pr.at[k], (partner, g))
        copy.start()
        pair.append(copy)
        if k == 0:
            load.wait()
        else:
            finish(k - 1)
    finish(half - 1)
    if not early:
        for copy in summed:
            copy.start()
    result = part[rows_at(g, here), :].astype(jnp.float32)
    for k in range(1, m):
        summed[k - 1].wait_recv()
        result = result + landed[k - 1].astype(jnp.float32)
    out_ref[...] = (res_ref[...].astype(jnp.float32) + result).astype(jnp.bfloat16)
    for copy in sends + cross + pair + summed:
        copy.wait_send()


def multiply(act, w_ref, part, copy, chip, rows):
    copy.wait_recv()
    block = act[pl.ds(chip * 2, 2)].reshape(2 * rows, act.shape[2])
    part[rows_at(chip, 2 * rows), :] = jnp.dot(
        block, w_ref[...], preferred_element_type=jnp.float32
    ).astype(jnp.bfloat16)


def output(n, m, collective_id, regroup, activity, weight, residual):
    here, features = residual.shape
    tokens = here * m
    rows = tokens // n
    half = n // 2
    dma = pltpu.SemaphoreType.DMA
    return pl.pallas_call(
        functools.partial(output_kernel, n, m, regroup),
        out_shape=jax.ShapeDtypeStruct((here, features), jnp.bfloat16),
        in_specs=[
            pl.BlockSpec(memory_space=pltpu.VMEM),
            pl.BlockSpec(memory_space=pl.ANY),
            pl.BlockSpec(memory_space=pltpu.VMEM),
        ],
        out_specs=pl.BlockSpec(memory_space=pltpu.VMEM),
        scratch_shapes=[
            pltpu.VMEM((n, rows, weight.shape[0]), jnp.bfloat16),
            pltpu.VMEM((tokens, features), jnp.bfloat16),
            pltpu.VMEM((m - 1, here, features), jnp.bfloat16),
            pltpu.VMEM(weight.shape, jnp.bfloat16),
            dma((m - 1,)), dma((m - 1,)),
            dma((half - 1,)), dma((half - 1,)),
            dma((half,)), dma((half,)),
            dma((m - 1,)), dma((m - 1,)),
            dma((1,)),
        ],
        compiler_params=pltpu.CompilerParams(
            collective_id=collective_id, has_side_effects=True, vmem_limit_bytes=VMEM_LIMIT
        ),
    )(activity, weight, residual)


def contract(left, right):
    return lax.dot_general(
        left, right, (((1,), (1,)), ((), ())), preferred_element_type=jnp.float32
    )


def attend_kernel(heads, own, q_ref, k_ref, v_ref, length_ref, out_ref):
    rows, slots, _ = k_ref.shape
    count = q_ref.shape[1]
    scale = HEAD_DIM ** (-0.5)
    shape = (count, rows * slots)
    row = lax.broadcasted_iota(jnp.int32, shape, 0) // NEW
    column = lax.broadcasted_iota(jnp.int32, shape, 1)
    slot = column - row * slots
    visible = (slot >= 0) & (slot < length_ref[...])
    if own:
        mine = (count, count)
        token = lax.broadcasted_iota(jnp.int32, mine, 0)
        key = lax.broadcasted_iota(jnp.int32, mine, 1)
        causal = (token // NEW == key // NEW) & (key <= token)
    for h in range(heads):
        span = pl.ds(h * HEAD_DIM, HEAD_DIM)
        query = q_ref[0, :, span]
        keys = k_ref[:, :, span].reshape(rows * slots, HEAD_DIM)
        values = v_ref[:, :, span].reshape(rows * slots, HEAD_DIM)
        exps = jnp.where(visible, jnp.exp(contract(query, keys) * scale), 0.0)
        totals = jnp.sum(exps, axis=1, keepdims=True)
        if own:
            new_keys = q_ref[0, :, pl.ds((heads + h) * HEAD_DIM, HEAD_DIM)]
            new_values = q_ref[0, :, pl.ds((2 * heads + h) * HEAD_DIM, HEAD_DIM)]
            fresh = jnp.where(causal, jnp.exp(contract(query, new_keys) * scale), 0.0)
            totals = totals + jnp.sum(fresh, axis=1, keepdims=True)
        mix = jnp.dot(
            (exps / totals).astype(jnp.bfloat16), values, preferred_element_type=jnp.float32
        )
        if own:
            mix = mix + jnp.dot(
                (fresh / totals).astype(jnp.bfloat16), new_values,
                preferred_element_type=jnp.float32,
            )
        out_ref[0, :, span] = mix.astype(jnp.bfloat16)


def attend(own, queries, keys, values, lengths):
    m, count, columns = queries.shape
    rows, slots, features = keys.shape
    width = features // m
    spread = jnp.repeat(lengths, count // rows).reshape(count, 1)
    return pl.pallas_call(
        functools.partial(attend_kernel, width // HEAD_DIM, own),
        out_shape=jax.ShapeDtypeStruct((m, count, width), jnp.bfloat16),
        grid=(m,),
        in_specs=[
            pl.BlockSpec((1, count, columns), lambda s: (s, 0, 0)),
            pl.BlockSpec((rows, slots, width), lambda s: (0, 0, s)),
            pl.BlockSpec((rows, slots, width), lambda s: (0, 0, s)),
            pl.BlockSpec((count, 1), lambda s: (0, 0)),
        ],
        out_specs=pl.BlockSpec((1, count, width), lambda s: (s, 0, 0)),
        compiler_params=pltpu.CompilerParams(vmem_limit_bytes=VMEM_LIMIT),
    )(queries, keys, values, spread)


def per_device(
    tokens,
    gains,
    w_qkv,
    w_self_out,
    w_cross_q,
    w_cross_out,
    w_ffn_in,
    w_ffn_out,
    self_keys,
    self_values,
    cross_keys,
    cross_values,
    positions,
    src_len,
):
    n, m = lax.axis_size("gx"), lax.axis_size("gy")
    stream = tokens.reshape(tokens.shape[0] * NEW, tokens.shape[2])
    projected = project(n, m, 0, False, stream, gains[0:1], jnp.transpose(w_qkv, (1, 0, 2)))
    mixed = attend(True, projected, self_keys, self_values, positions)
    after_self = output(n, m, 1, True, mixed, w_self_out, stream)
    queries = project(n, m, 2, False, after_self, gains[1:2], w_cross_q[None])
    crossed = attend(False, queries, cross_keys, cross_values, src_len)
    after_cross = output(n, m, 3, True, crossed, w_cross_out, after_self)
    hidden = project(
        n, m, 4, True, after_cross, gains[2:3], jnp.transpose(w_ffn_in, (1, 0, 2))
    )
    result = output(n, m, 5, False, hidden, w_ffn_out, after_cross)
    return result.reshape(tokens.shape)


def solution(mesh):
    return jax.shard_map(
        per_device,
        mesh=mesh,
        in_specs=(
            P("gy", None, "gx"),
            P(None, "gx"),
            P("gx", None, "gy"),
            P("gy", "gx"),
            P("gx", "gy"),
            P("gy", "gx"),
            P("gx", None, "gy"),
            P("gy", "gx"),
            P(("gx", "gy"), None, None),
            P(("gx", "gy"), None, None),
            P(("gx", "gy"), None, None),
            P(("gx", "gy"), None, None),
            P(("gx", "gy")),
            P(("gx", "gy")),
        ),
        out_specs=P("gy", None, "gx"),
        check_vma=False,
    )
```
